32 devices in a mesh: row: 4 (over y, x), sub: 8 (over z, core).
Axes of the slice: x: 2, y: 2, z: 4, core: 2. Of those that a mesh axis runs over, the one named last changes fastest.
Arguments:
- ritz_coefficients: bfloat16 [4096, 2048], P('row', 'sub'), may hold values from -6 to 6
- mode_map: int32 [32, 128], P(('row', 'sub')), may hold values from 0 to 127, each once within a row
- leaf_count: int32 [32], P(('row', 'sub')), may hold values from 24 to 48, as said below
- mode_blocks: bfloat16 [33280, 2048], P(('row', 'sub'))
Outputs:
- eigenvectors: bfloat16 [65536, 2048], P(('row', 'sub'))
The draws below stay inside these ranges and needn't reach their ends.
Inputs may be any that keep to these rules, and one draw needn't show every extreme that they name: `mode_map`: each row is a permutation of 0 to 127. `leaf_count`: some substructure uses all 48 interior modes.
All inputs are finite; a program needn't handle non-finite values.
Results may differ from the reference program's by a relative error of at most 0.001.
Values may be sent and summed in bfloat16 or wider, within the bound.
A program may use at most 64 MiB of HBM per device.

```python
import jax
import jax.numpy as jnp
from jax import lax

NEV = 2048
KM = 128
SR = 16
LEVELS = 5
NDOF = 2048
LM = 48
MCOLS = 1040
NSUBS = 32
K = 4096


def draw_leaf_count(key, part):
    counts = jax.random.randint(key, (NSUBS,), LM // 2, LM + 1)
    position = jax.random.randint(jax.random.fold_in(key, 7), (), 0, NSUBS)
    return counts.at[position].set(LM).astype(jnp.int32)


def draw_mode_blocks(key, part):
    total_rows = NSUBS * MCOLS
    column = jnp.arange(total_rows, dtype=jnp.int32) % MCOLS
    offset = column - LM
    level_number = jnp.ones_like(offset)
    for extra in range(2, LEVELS + 1):
        level_number = level_number + (offset >= SR * (2 ** extra - 2)).astype(jnp.int32)
    separator_rows = SR * jnp.left_shift(jnp.ones_like(level_number), level_number)
    fan_in = jnp.where(offset < 0, LM, separator_rows).astype(jnp.float32)
    row_scale = 1.0 / jnp.sqrt(fan_in * (LEVELS + 1.0))
    values = jax.random.normal(key, (total_rows, NDOF), jnp.float32)
    return (values * row_scale[:, None]).astype(jnp.bfloat16)


def levels(key, shape, cuts, least, largest):
    factor_of, own = 1.0, jax.random.fold_in(key, 6)
    for dim, shards_of in cuts:
        draws = jnp.exp(jax.random.uniform(jax.random.fold_in(own, dim), (shards_of,), jnp.float32, least / len(cuts), largest / len(cuts)))
        factor_of = factor_of * jnp.repeat(draws, shape[dim] // shards_of).reshape([-1 if axis == dim else 1 for axis in range(len(shape))])
    return factor_of


def bell_draw(stream_key, extent, deviation, most, split=(), kind=jnp.bfloat16):
    entries = deviation * jax.random.normal(stream_key, extent, jnp.float32)
    if split:
        entries = entries * levels(stream_key, extent, split, -0.22, 0.18)
    return jnp.clip(entries, -most, most).astype(kind)


def setup_inputs(seed: int = 0) -> dict:
    key_of = jax.random.split(jax.random.key(seed), 5)
    ritz_coefficients = bell_draw(key_of[0], (K, NEV), 1.0, 6.0, ((0, 4), (1, 8)))
    mode_map = jax.vmap(lambda own: jax.random.permutation(own, KM))(jax.random.split(key_of[1], NSUBS)).reshape((NSUBS, KM)).astype(jnp.int32)
    leaf_count = draw_leaf_count(jax.random.fold_in(key_of[4], 71), 0)
    mode_blocks = draw_mode_blocks(jax.random.fold_in(key_of[4], 71), 0)
    return dict(ritz_coefficients=ritz_coefficients, mode_map=mode_map, leaf_count=leaf_count, mode_blocks=mode_blocks)


def reference(ritz_coefficients, mode_map, leaf_count, mode_blocks):
    lanczos_rows = ritz_coefficients.reshape(NSUBS, KM, NEV)

    def place_rows(pair):
        source_rows, slot_order = pair
        return jnp.zeros((KM, NEV), jnp.bfloat16).at[slot_order].set(source_rows)

    coeffs = lax.map(place_rows, (lanczos_rows, mode_map))
    kept_rows = jnp.arange(LM, dtype=jnp.int32)[None, :] < leaf_count[:, None]
    leaf_rows = jnp.where(kept_rows[:, :, None], coeffs[:, :LM], jnp.zeros((), jnp.bfloat16))
    grouped = []
    for level_number in range(1, LEVELS + 1):
        own_share = coeffs[:, LM + (level_number - 1) * SR: LM + level_number * SR]
        grouped.append(own_share.reshape(NSUBS >> level_number, (2 ** level_number) * SR, NEV))
    blocks = mode_blocks.reshape(NSUBS, MCOLS, NDOF)

    def recover(triple):
        modes_block, own_leaf, device = triple
        pieces = [own_leaf]
        for level_number in range(1, LEVELS + 1):
            pieces.append(lax.dynamic_index_in_dim(grouped[level_number - 1], device >> level_number, 0, keepdims=False))
        all_coeffs = jnp.concatenate(pieces, axis=0)
        product = lax.dot_general(modes_block, all_coeffs, (((0,), (0,)), ((), ())), preferred_element_type=jnp.float32)
        return product.astype(jnp.bfloat16)

    result = lax.map(recover, (blocks, leaf_rows, jnp.arange(NSUBS, dtype=jnp.int32)))
    return result.reshape(NSUBS * NDOF, NEV)
```

```python
import functools

import jax
import jax.numpy as jnp
from jax import lax
from jax.experimental import pallas as pl
from jax.experimental.pallas import tpu as pltpu
from jax.sharding import PartitionSpec as P

SR = 16
LEVELS = 5
MESH = pl.DeviceIdType.MESH


def gather_kernel(R, S, leaf, ritz, maps_in, out, maps, leaves, shares, map_s, map_r, loc_s,
                  leaf_s, leaf_r, near_s, near_r, line_s, line_r, row_s, row_r, sib_s, sib_r):
    kept, width = leaf + LEVELS * SR, ritz.shape[1]
    Z = S // 2
    sub_bits = S.bit_length() - 1
    low = min(sub_bits - 1, LEVELS)
    wide = range(sub_bits, LEVELS + 1)
    row_bits = max(LEVELS - sub_bits, 0)
    seg = SR * S
    r, s = lax.axis_index("row"), lax.axis_index("sub")
    z, core = s // 2, s % 2
    cols = out.shape[1]

    def offset(l):
        return leaf + SR * (2**l - 2)

    def col(k):
        return 2 * k + core

    def remote(src, dst, ssem, rsem, row=None, sub=None):
        return pltpu.make_async_remote_copy(
            src_ref=src, dst_ref=dst, send_sem=ssem, recv_sem=rsem,
            device_id=(r if row is None else row, s if sub is None else sub), device_id_type=MESH)

    def partner(b):
        bit = (r // (1 << b)) % 2
        return r + (1 - 2 * bit) * (1 << b)

    barrier = pltpu.get_barrier_semaphore()
    for d in range(1, S):
        pl.semaphore_signal(barrier, inc=1, device_id=(r, (s + d) % S), device_id_type=MESH)
    for b in range(row_bits):
        pl.semaphore_signal(barrier, inc=1, device_id=(partner(b), s), device_id_type=MESH)
    pl.semaphore_wait(barrier, S - 1 + row_bits)

    def map_copy(d):
        t = (s + d) % S
        return remote(maps_in, maps.at[s], map_s.at[d], map_r.at[d], sub=t)

    for d in range(1, S):
        map_copy(d).start()
    maps[s] = maps_in[...]
    for d in range(1, S):
        map_copy(d).wait_recv()

    slot = lax.broadcasted_iota(jnp.int32, (kept, kept), 0)
    for t in range(S):
        table = (slot == maps[t]).astype(jnp.float32).astype(jnp.bfloat16)
        placed = jnp.dot(table, ritz[t * kept:(t + 1) * kept, :], preferred_element_type=jnp.float32)
        placed = placed.astype(jnp.bfloat16)
        leaves[t] = placed[:leaf]
        for l in range(LEVELS):
            shares[l, t * SR:(t + 1) * SR] = placed[leaf + l * SR:leaf + (l + 1) * SR]

    def rows(k, start, size):
        return out.at[k, pl.ds(pl.multiple_of(start, 16), size)]

    def own_rows(l, b=0):
        span = max(1 << (l - sub_bits), 1)
        return offset(l) + (r % span) // (1 << b) * (seg << b), seg << b

    def group(l, k):
        return shares.at[l - 1, pl.ds(pl.multiple_of((2 * k) // (1 << l) * (SR << l), 16), SR << l)]

    local = [pltpu.make_async_copy(leaves.at[s], rows(s, 0, leaf), loc_s.at[0])]
    for l in range(1, low + 1):
        local.append(pltpu.make_async_copy(group(l, z), rows(s, offset(l), SR << l), loc_s.at[l]))
    for l in wide:
        start, size = own_rows(l)
        local.append(pltpu.make_async_copy(shares.at[l - 1], rows(s, start, size), loc_s.at[l]))

    def line_copy(k, way, l, first=False):
        start, size = own_rows(l)
        place = rows(col(k), start, size)
        src = shares.at[l - 1] if first else place
        j = l - sub_bits
        return remote(src, place, line_s.at[way, k, j], line_r.at[k, j], sub=s + (2 if way else -2))

    def row_copy(k, b, l, first=False):
        start, size = own_rows(l, b)
        place = rows(col(k), start, size)
        src = shares.at[l - 1] if first else place
        j = l - sub_bits - 1
        return remote(src, place, row_s.at[k, b, j], row_r.at[k, b, j], row=partner(b))

    def row_arrival(k, b, l):
        span = 1 << (l - sub_bits)
        start = offset(l) + (partner(b) % span) // (1 << b) * (seg << b)
        place = rows(col(k), start, seg << b)
        j = l - sub_bits - 1
        return remote(place, place, row_s.at[k, b, j], row_r.at[k, b, j], row=partner(b))

    def near_copy(d, l):
        k = (z + d) % Z
        return remote(group(l, k), rows(s, offset(l), SR << l), near_s.at[d, l - 1],
                      near_r.at[d, l - 1], sub=2 * k + core)

    def near_arrival(d, l):
        k = (z + Z - d) % Z
        place = rows(col(k), offset(l), SR << l)
        return remote(place, place, near_s.at[d, l - 1], near_r.at[d, l - 1], sub=col(k))

    def leaf_copy(d):
        t = (s + d) % S
        return remote(leaves.at[t], rows(s, 0, leaf), leaf_s.at[d], leaf_r.at[d], sub=t)

    def leaf_arrival(d):
        t = (s + S - d) % S
        return remote(rows(t, 0, leaf), rows(t, 0, leaf), leaf_s.at[d], leaf_r.at[d], sub=t)

    def sib_copy(k, mine=True):
        c = 2 * k + (core if mine else 1 - core)
        place = rows(c, leaf, cols - leaf)
        return remote(place, place, sib_s.at[k], sib_r.at[k], sub=2 * z + 1 - core)

    def each(t, f):
        if t == 0:
            f(z, None)
        else:
            pl.when(z >= t)(lambda: f(z - t, 1))
            pl.when(z + t < Z)(lambda: f(z + t, 0))

    def guarded(way, f):
        pl.when((z + 1 < Z) if way else (z >= 1))(f)

    def line_step(t):
        def f(k, way):
            if way is not None:
                for l in wide:
                    line_copy(k, way, l).wait_recv()
            for w in ((0, 1) if way is None else (way,)):
                def send():
                    for l in reversed(wide):
                        line_copy(k, w, l, t == 0).start()
                guarded(w, send)
            for l in range(sub_bits + 1, LEVELS + 1):
                row_copy(k, 0, l, t == 0).start()
        each(t, f)

    def row_step(t, b):
        def f(k, way):
            for l in range(sub_bits + b, LEVELS + 1):
                row_arrival(k, b - 1, l).wait_recv()
            for l in range(sub_bits + b + 1, LEVELS + 1):
                row_copy(k, b, l).start()
        each(t, f)

    def sib_step(t):
        each(t, lambda k, way: sib_copy(k).start())

    line_step(0)
    for c in local:
        c.start()
    for d in range(1, Z):
        for l in range(1, low + 1):
            near_copy(d, l).start()
    for d in range(1, S):
        leaf_copy(d).start()
    for c in local:
        c.wait()
    for tick in range(1, Z + row_bits):
        if tick < Z:
            line_step(tick)
        for b in range(1, row_bits + 1):
            if 0 <= tick - b < Z:
                row_step(tick - b, b)
        if tick == 1:
            for d in range(1, Z):
                for l in range(1, low + 1):
                    near_arrival(d, l).wait_recv()
        if 0 <= tick - row_bits < Z:
            sib_step(tick - row_bits)
    for k in range(Z):
        sib_copy(k, False).wait_recv()
    for d in range(1, S):
        leaf_arrival(d).wait_recv()

    def drain(t):
        def f(k, way):
            for w in ((0, 1) if way is None else (way,)):
                def left():
                    for l in wide:
                        line_copy(k, w, l).wait_send()
                guarded(w, left)
            for b in range(row_bits):
                for l in range(sub_bits + b + 1, LEVELS + 1):
                    row_copy(k, b, l).wait_send()
            sib_copy(k).wait_send()
        each(t, f)

    for t in range(Z):
        drain(t)
    for d in range(1, Z):
        for l in range(1, low + 1):
            near_copy(d, l).wait_send()
    for d in range(1, S):
        leaf_copy(d).wait_send()
        map_copy(d).wait_send()


def recover_kernel(leaf, count, modes, coeffs, out, turned):
    @pl.when(pl.program_id(0) == 0)
    def _():
        ndof = modes.shape[1]
        part = 256
        row = lax.broadcasted_iota(jnp.int32, (modes.shape[0], part), 0)

        @pl.loop(0, ndof // part)
        def _(i):
            at = pl.ds(pl.multiple_of(i * part, part), part)
            block = modes[:, at].astype(jnp.float32)
            block = jnp.where((row < leaf) & (row >= count[0]), 0.0, block)
            turned[at, :] = block.T.astype(jnp.bfloat16)

    out[...] = jnp.dot(turned[...], coeffs[0], preferred_element_type=jnp.float32).astype(jnp.bfloat16)


def shards(R, S, ritz_coefficients, mode_map, leaf_count, mode_blocks):
    kept = mode_map.shape[1]
    leaf = kept - LEVELS * SR
    width = ritz_coefficients.shape[1]
    cols, ndof = mode_blocks.shape
    Z = S // 2
    sub_bits = S.bit_length() - 1
    row_bits = max(LEVELS - sub_bits, 1)
    dma = pltpu.SemaphoreType.DMA
    coeffs = pl.pallas_call(
        functools.partial(gather_kernel, R, S, leaf),
        out_shape=jax.ShapeDtypeStruct((S, cols, width), jnp.bfloat16),
        in_specs=[pl.BlockSpec(memory_space=pltpu.VMEM)] * 2,
        out_specs=pl.BlockSpec(memory_space=pl.ANY),
        scratch_shapes=[
            pltpu.VMEM((S, 1, kept), jnp.int32),
            pltpu.VMEM((S, leaf, width), jnp.bfloat16),
            pltpu.VMEM((LEVELS, S * SR, width), jnp.bfloat16),
            dma((S,)), dma((S,)),
            dma((LEVELS + 1,)),
            dma((S,)), dma((S,)),
            dma((Z, sub_bits)), dma((Z, sub_bits)),
            dma((2, Z, LEVELS)), dma((Z, LEVELS)),
            dma((Z, row_bits, row_bits)), dma((Z, row_bits, row_bits)),
            dma((Z,)), dma((Z,)),
        ],
        compiler_params=pltpu.CompilerParams(
            collective_id=0, has_side_effects=True, vmem_limit_bytes=32 << 20),
    )(ritz_coefficients, mode_map)
    return pl.pallas_call(
        functools.partial(recover_kernel, leaf),
        grid=(S,),
        out_shape=jax.ShapeDtypeStruct((ndof, S * width), jnp.bfloat16),
        in_specs=[
            pl.BlockSpec(memory_space=pltpu.SMEM),
            pl.BlockSpec((cols, ndof), lambda n: (0, 0)),
            pl.BlockSpec((1, cols, width), lambda n: (n, 0, 0)),
        ],
        out_specs=pl.BlockSpec((ndof, width), lambda n: (0, n)),
        scratch_shapes=[pltpu.VMEM((ndof, cols), jnp.bfloat16)],
        compiler_params=pltpu.CompilerParams(vmem_limit_bytes=48 << 20),
    )(leaf_count, mode_blocks, coeffs)


def solution(mesh):
    return jax.shard_map(
        functools.partial(shards, mesh.shape["row"], mesh.shape["sub"]),
        mesh=mesh,
        in_specs=(
            P("row", "sub"),
            P(("row", "sub"), None),
            P(("row", "sub")),
            P(("row", "sub"), None),
        ),
        out_specs=P(("row", "sub"), None),
        check_vma=False,
    )
```

```python
import functools

import jax
import jax.numpy as jnp
from jax import lax
from jax.experimental import pallas as pl
from jax.experimental.pallas import tpu as pltpu
from jax.sharding import PartitionSpec as P

SR = 16
LEVELS = 5
MESH = pl.DeviceIdType.MESH
PERSONAL = 2


def gather_kernel(R, S, leaf, count, ritz_in, maps_in, modes_in, out, turned_out, ritz, modes, turned,
                  maps, leaves, shares, load_s, turn_s, map_s, map_r, loc_s, leaf_s, leaf_r, near_s, near_r, line_s, line_r, row_s, row_r, sib_s, sib_r):
    kept, width = leaf + LEVELS * SR, ritz.shape[1]
    Z = S // 2
    sub_bits = S.bit_length() - 1
    low = min(sub_bits - 1, LEVELS)
    wide = range(sub_bits, LEVELS + 1)
    row_bits = max(LEVELS - sub_bits, 0)
    seg = SR * S
    r, s = lax.axis_index("row"), lax.axis_index("sub")
    z, core = s // 2, s % 2
    cols = out.shape[1]

    def offset(l):
        return leaf + SR * (2**l - 2)

    def col(k):
        return 2 * k + core

    def remote(src, dst, ssem, rsem, row=None, sub=None):
        return pltpu.make_async_remote_copy(
            src_ref=src, dst_ref=dst, send_sem=ssem, recv_sem=rsem,
            device_id=(r if row is None else row, s if sub is None else sub), device_id_type=MESH)

    def partner(b):
        bit = (r // (1 << b)) % 2
        return r + (1 - 2 * bit) * (1 << b)

    loads = [pltpu.make_async_copy(ritz_in, ritz, load_s.at[0]),
             pltpu.make_async_copy(maps_in, maps.at[s], load_s.at[1]),
             pltpu.make_async_copy(modes_in, modes, load_s.at[2])]
    for c in loads:
        c.start()

    barrier = pltpu.get_barrier_semaphore()
    for d in range(1, S):
        pl.semaphore_signal(barrier, inc=1, device_id=(r, (s + d) % S), device_id_type=MESH)
    for b in range(row_bits):
        pl.semaphore_signal(barrier, inc=1, device_id=(partner(b), s), device_id_type=MESH)
    pl.semaphore_wait(barrier, S - 1 + row_bits)

    def map_copy(d):
        t = (s + d) % S
        return remote(maps.at[s], maps.at[s], map_s.at[d], map_r.at[d], sub=t)

    loads[1].wait()
    for d in range(1, S):
        map_copy(d).start()
    loads[0].wait()
    for d in range(1, S):
        map_copy(d).wait_recv()

    slot = lax.broadcasted_iota(jnp.int32, (kept, kept), 0)
    for t in range(S):
        table = (slot == maps[t]).astype(jnp.float32).astype(jnp.bfloat16)
        placed = jnp.dot(table, ritz[t * kept:(t + 1) * kept, :], preferred_element_type=jnp.float32)
        placed = placed.astype(jnp.bfloat16)
        leaves[t] = placed[:leaf]
        for l in range(LEVELS):
            shares[l, t * SR:(t + 1) * SR] = placed[leaf + l * SR:leaf + (l + 1) * SR]

    def rows(k, start, size):
        return out.at[k, pl.ds(pl.multiple_of(start, 16), size)]

    def own_rows(l, b=0):
        span = max(1 << (l - sub_bits), 1)
        return offset(l) + (r % span) // (1 << b) * (seg << b), seg << b

    def group(l, k):
        return shares.at[l - 1, pl.ds(pl.multiple_of((2 * k) // (1 << l) * (SR << l), 16), SR << l)]

    local = [pltpu.make_async_copy(leaves.at[s], rows(s, 0, leaf), loc_s.at[0])]
    for l in range(1, low + 1):
        local.append(pltpu.make_async_copy(group(l, z), rows(s, offset(l), SR << l), loc_s.at[l]))
    for l in wide:
        start, size = own_rows(l)
        local.append(pltpu.make_async_copy(shares.at[l - 1], rows(s, start, size), loc_s.at[l]))

    def line_copy(k, way, l, first=False):
        start, size = own_rows(l)
        place = rows(col(k), start, size)
        src = shares.at[l - 1] if first else place
        j = l - sub_bits
        return remote(src, place, line_s.at[way, k, j], line_r.at[k, j], sub=s + (2 if way else -2))

    def row_copy(k, b, l, first=False):
        start, size = own_rows(l, b)
        place = rows(col(k), start, size)
        src = shares.at[l - 1] if first else place
        j = l - sub_bits - 1
        return remote(src, place, row_s.at[k, b, j], row_r.at[k, b, j], row=partner(b))

    def row_arrival(k, b, l):
        span = 1 << (l - sub_bits)
        start = offset(l) + (partner(b) % span) // (1 << b) * (seg << b)
        place = rows(col(k), start, seg << b)
        j = l - sub_bits - 1
        return remote(place, place, row_s.at[k, b, j], row_r.at[k, b, j], row=partner(b))

    def near_copy(d, l):
        k = (z + d) % Z
        return remote(group(l, k), rows(s, offset(l), SR << l), near_s.at[d, l - 1],
                      near_r.at[d, l - 1], sub=2 * k + core)

    def near_arrival(d, l):
        k = (z + Z - d) % Z
        place = rows(col(k), offset(l), SR << l)
        return remote(place, place, near_s.at[d, l - 1], near_r.at[d, l - 1], sub=col(k))

    def leaf_copy(d):
        t = (s + d) % S
        return remote(leaves.at[t], rows(s, 0, leaf), leaf_s.at[d], leaf_r.at[d], sub=t)

    def leaf_arrival(d):
        t = (s + S - d) % S
        return remote(rows(t, 0, leaf), rows(t, 0, leaf), leaf_s.at[d], leaf_r.at[d], sub=t)

    def sib_copy(k, mine=True):
        c = 2 * k + (core if mine else 1 - core)
        place = rows(c, leaf, cols - leaf)
        return remote(place, place, sib_s.at[k], sib_r.at[k], sub=2 * z + 1 - core)

    def each(t, f):
        if t == 0:
            f(z, None)
        else:
            pl.when(z >= t)(lambda: f(z - t, 1))
            pl.when(z + t < Z)(lambda: f(z + t, 0))

    def guarded(way, f):
        pl.when((z + 1 < Z) if way else (z >= 1))(f)

    def line_step(t, levels):
        for l in levels:
            line_level(t, l)

    def line_level(t, l):
        def f(k, way):
            if True:
                if way is not None:
                    line_copy(k, way, l).wait_recv()
                for w in ((0, 1) if way is None else (way,)):
                    guarded(w, lambda w=w: line_copy(k, w, l, t == 0).start())
                if l > sub_bits:
                    row_copy(k, 0, l, t == 0).start()
        each(t, f)

    def row_step(t, b):
        def f(k, way):
            for l in range(sub_bits + b, LEVELS + 1):
                row_arrival(k, b - 1, l).wait_recv()
            for l in range(sub_bits + b + 1, LEVELS + 1):
                row_copy(k, b, l).start()
        each(t, f)

    def last_row(t):
        def f(k, way):
            for l in range(sub_bits + row_bits, LEVELS + 1):
                row_arrival(k, row_bits - 1, l).wait_recv()
        each(t, f)

    def sib_step(t):
        each(t, lambda k, way: sib_copy(k).start())

    parts = 2 * Z
    part = modes.shape[1] // parts

    def turn(i):
        if i == 0:
            loads[2].wait()
        row = lax.broadcasted_iota(jnp.int32, (cols, part), 0)
        block = modes[:, i * part:(i + 1) * part].astype(jnp.float32)
        block = jnp.where((row < leaf) & (row >= count[0]), 0.0, block)
        turned[i * part:(i + 1) * part, :] = block.T.astype(jnp.bfloat16)
        turn_copy(i).start()

    def turn_copy(i):
        at = pl.ds(i * part, part)
        return pltpu.make_async_copy(turned.at[at], turned_out.at[at], turn_s.at[i])

    upper = tuple(reversed(range(sub_bits + 1, LEVELS + 1)))
    line_step(0, upper)
    for c in local:
        c.start()
    line_step(0, (sub_bits,))
    for c in local:
        c.wait()
    done = 0
    for tick in range(1, Z + row_bits + 1):
        if done < parts:
            for i in range(done, done + 2):
                turn(i)
            done += 2
        if tick < Z:
            line_step(tick, upper)
        for b in range(1, row_bits):
            if 0 <= tick - b < Z:
                row_step(tick - b, b)
        if 1 <= tick - 1 < Z:
            line_step(tick - 1, (sub_bits,))
        if tick == PERSONAL:
            for d in range(1, Z):
                for l in range(1, low + 1):
                    near_copy(d, l).start()
            for d in range(1, S):
                leaf_copy(d).start()
        if tick == Z:
            for d in range(1, Z):
                for l in range(1, low + 1):
                    near_arrival(d, l).wait_recv()
        if tick >= Z:
            for t in (range(tick - row_bits + 1) if tick == Z else (tick - row_bits,)):
                if t < Z:
                    last_row(t)
                    sib_step(t)
    for i in range(parts):
        turn_copy(i).wait()
    for k in range(Z):
        sib_copy(k, False).wait_recv()
    for d in range(1, S):
        leaf_arrival(d).wait_recv()

    def drain(t):
        def f(k, way):
            for w in ((0, 1) if way is None else (way,)):
                def left():
                    for l in wide:
                        line_copy(k, w, l).wait_send()
                guarded(w, left)
            for b in range(row_bits):
                for l in range(sub_bits + b + 1, LEVELS + 1):
                    row_copy(k, b, l).wait_send()
            sib_copy(k).wait_send()
        each(t, f)

    for t in range(Z):
        drain(t)
    for d in range(1, Z):
        for l in range(1, low + 1):
            near_copy(d, l).wait_send()
    for d in range(1, S):
        leaf_copy(d).wait_send()
        map_copy(d).wait_send()


def recover_kernel(turned, coeffs, out):
    out[...] = jnp.dot(turned[...], coeffs[0], preferred_element_type=jnp.float32).astype(jnp.bfloat16)


def shards(R, S, ritz_coefficients, mode_map, leaf_count, mode_blocks):
    kept = mode_map.shape[1]
    leaf = kept - LEVELS * SR
    width = ritz_coefficients.shape[1]
    cols, ndof = mode_blocks.shape
    Z = S // 2
    sub_bits = S.bit_length() - 1
    row_bits = max(LEVELS - sub_bits, 1)
    dma = pltpu.SemaphoreType.DMA
    coeffs, turned = pl.pallas_call(
        functools.partial(gather_kernel, R, S, leaf),
        out_shape=[jax.ShapeDtypeStruct((S, cols, width), jnp.bfloat16),
                   jax.ShapeDtypeStruct((ndof, cols), jnp.bfloat16)],
        in_specs=[pl.BlockSpec(memory_space=pltpu.SMEM)] + [pl.BlockSpec(memory_space=pl.ANY)] * 3,
        out_specs=[pl.BlockSpec(memory_space=pl.ANY)] * 2,
        scratch_shapes=[
            pltpu.VMEM(ritz_coefficients.shape, jnp.bfloat16),
            pltpu.VMEM((cols, ndof), jnp.bfloat16),
            pltpu.VMEM((ndof, cols), jnp.bfloat16),
            pltpu.VMEM((S, 1, kept), jnp.int32),
            pltpu.VMEM((S, leaf, width), jnp.bfloat16),
            pltpu.VMEM((LEVELS, S * SR, width), jnp.bfloat16),
            dma((3,)), dma((S,)),
            dma((S,)), dma((S,)),
            dma((LEVELS + 1,)),
            dma((S,)), dma((S,)),
            dma((Z, sub_bits)), dma((Z, sub_bits)),
            dma((2, Z, LEVELS)), dma((Z, LEVELS)),
            dma((Z, row_bits, row_bits)), dma((Z, row_bits, row_bits)),
            dma((Z,)), dma((Z,)),
        ],
        compiler_params=pltpu.CompilerParams(
            collective_id=0, has_side_effects=True, vmem_limit_bytes=60 << 20),
    )(leaf_count, ritz_coefficients, mode_map, mode_blocks)
    return pl.pallas_call(
        recover_kernel,
        grid=(S,),
        out_shape=jax.ShapeDtypeStruct((ndof, S * width), jnp.bfloat16),
        in_specs=[
            pl.BlockSpec((ndof, cols), lambda n: (0, 0)),
            pl.BlockSpec((1, cols, width), lambda n: (n, 0, 0)),
        ],
        out_specs=pl.BlockSpec((ndof, width), lambda n: (0, n)),
        compiler_params=pltpu.CompilerParams(vmem_limit_bytes=60 << 20),
    )(turned, coeffs)


def solution(mesh):
    return jax.shard_map(
        functools.partial(shards, mesh.shape["row"], mesh.shape["sub"]),
        mesh=mesh,
        in_specs=(
            P("row", "sub"),
            P(("row", "sub"), None),
            P(("row", "sub")),
            P(("row", "sub"), None),
        ),
        out_specs=P(("row", "sub"), None),
        check_vma=False,
    )
```
